32 devices in a mesh: parts: 2 (over y), tensor: 2 (over x), dp: 8 (over z, core).
Axes of the slice: x: 2, y: 2, z: 4, core: 2. Of those that a mesh axis runs over, the one named last changes fastest.
Arguments:
- activations: bfloat16 [48, 512, 28672], P(('parts', 'dp'), None, 'tensor'), parts along dimension 0, may hold values from -6 to 6
- out_grads: bfloat16 [48, 512, 8192], P(('parts', 'dp'), None, 'tensor'), parts along dimension 0, may hold values from -6 to 6
- proj_in: bfloat16 [28672, 64], P('tensor'), may hold values from -0.03125 to 0.03125
- proj_out: bfloat16 [8192, 64], P('tensor'), may hold values from -0.0625 to 0.0625
- fisher_prior: float32 [4096, 4096], P('tensor'), as said below
- test_grads: float32 [256, 4096], P(('parts', 'dp')), parts along dimension 0, may hold values from -6 to 6
Outputs:
- scores: float32 [48, 128], P(('parts', 'dp')), parts along dimension 0
- preconditioned: float32 [256, 4096], P('parts', 'tensor'), parts along dimension 0
The draws below stay inside these ranges and needn't reach their ends.
There are 2 independent parts, one for each index of `parts`. The reference program is written for one: setup_inputs(seed, part) draws one part's arguments, and reference() takes and returns one part's arrays. A program takes and returns all parts, laid end to end along the dimension named above; an argument that names none is the same for every part. Nothing has to cross between parts.
Inputs may be any that keep to these rules, and one draw needn't show every extreme that they name: `fisher_prior`: the prior is symmetric.
All inputs are finite; a program needn't handle non-finite values.
Results may differ from the reference program's by a relative error of at most 0.0003.
Values sent between devices are 32-bit elements; how exact they have to be, the bound alone decides.
A program may use at most 320 MiB of HBM per device.

```python
import math
import jax
import jax.numpy as jnp
from jax import lax

D = 8192
FF = 28672
R = 64
K = 4096
LEN = 512
ITERS = 4
EXAMPLES = 24
TEST = 128


def draw_fisher_prior(key, part):
    key = jax.random.fold_in(key, 7)
    key_off, key_diag = jax.random.split(key)
    entries = jax.random.uniform(key_off, (K, K), jnp.float32, -1.0, 1.0)
    offdiag = (entries + entries.T) * (0.7 / math.sqrt(K))
    spread = jnp.exp(jax.random.uniform(key_diag, (K,), jnp.float32, jnp.log(0.2), jnp.log(6.0)))
    identity = jnp.eye(K, dtype=jnp.float32)
    return offdiag * (1.0 - identity) + identity * (1.6 + spread)[:, None]


def level_of(own_key, extent, cuts, smallest, largest):
    factor_of = 1.0
    for position, blocks in cuts:
        heights = jax.random.uniform(jax.random.fold_in(jax.random.fold_in(own_key, 6), position), (blocks,), jnp.float32, smallest / len(cuts), largest / len(cuts))
        factor_of = factor_of * jnp.repeat(jnp.exp(heights), extent[position] // blocks).reshape((-1,) + (1,) * (len(extent) - 1 - position))
    return factor_of


def centred(key, shape, scale, most, cuts=(), kind=jnp.bfloat16):
    drawn = scale * jax.random.normal(key, shape, jnp.float32)
    if cuts:
        drawn = drawn * level_of(key, shape, cuts, -0.22, 0.18)
    return jnp.clip(drawn, -most, most).astype(kind)


def setup_inputs(seed: int = 0, part: int = 0) -> dict:
    arg_keys = jax.random.split(jax.random.key(seed), 7)
    part_keys = jax.random.split(jax.random.fold_in(arg_keys[6], part), 7)
    activations = centred(part_keys[0], (EXAMPLES, LEN, FF), 1.0, 6.0, ((0, 8), (2, 2)))
    out_grads = centred(part_keys[1], (EXAMPLES, LEN, D), 1.0, 6.0, ((0, 8), (2, 2)))
    proj_in = centred(arg_keys[2], (FF, R), FF ** -0.5, 0.03125, ((0, 2),))
    proj_out = centred(arg_keys[3], (D, R), D ** -0.5, 0.0625, ((0, 2),))
    fisher_prior = draw_fisher_prior(jax.random.fold_in(arg_keys[6], 71), part)
    test_grads = centred(part_keys[5], (TEST, K), 1.0, 6.0, ((0, 8),), jnp.float32)
    return {"activations": activations, "out_grads": out_grads, "proj_in": proj_in, "proj_out": proj_out, "fisher_prior": fisher_prior, "test_grads": test_grads}


DAMPING = 0.1


def project_grads(act_proj, grad_proj):
    products = jnp.einsum("eto,eti->eoi", grad_proj, act_proj, precision=lax.Precision.HIGHEST)
    return products.reshape(products.shape[0], -1) / LEN


def reference(activations, out_grads, proj_in, proj_out, fisher_prior, test_grads):
    batch_rows, length_tok, width_ff = activations.shape
    width_model = out_grads.shape[2]
    act_proj = jnp.dot(activations.reshape(-1, width_ff), proj_in, preferred_element_type=jnp.float32).reshape(batch_rows, length_tok, -1)
    grad_proj = jnp.dot(out_grads.reshape(-1, width_model), proj_out, preferred_element_type=jnp.float32).reshape(batch_rows, length_tok, -1)
    gradients = project_grads(act_proj, grad_proj)
    fisher = fisher_prior + jnp.dot(gradients.T, gradients, precision=lax.Precision.HIGHEST)
    solution = jnp.zeros_like(test_grads)
    residual = test_grads
    direction = test_grads
    norm_now = jnp.sum(residual * residual, axis=1)
    for iteration in range(ITERS):
        applied = DAMPING * direction + jnp.dot(direction, fisher.T, precision=lax.Precision.HIGHEST)
        step_size = norm_now / jnp.sum(direction * applied, axis=1)
        solution = solution + step_size[:, None] * direction
        residual = residual - step_size[:, None] * applied
        norm_next = jnp.sum(residual * residual, axis=1)
        direction = residual + (norm_next / norm_now)[:, None] * direction
        norm_now = norm_next
    scores = jnp.dot(gradients, solution.T, precision=lax.Precision.HIGHEST)
    return scores, solution
```

```python
import jax
import jax.numpy as jnp
from jax import lax
from jax.sharding import PartitionSpec as P

LEN = 512
ITERS = 4
DAMPING = 0.1
CONTRACT = (((1,), (1,)), ((), ()))
HIGH = lax.Precision.HIGH


def shards(activations, out_grads, proj_in, proj_out, fisher_prior, test_grads):
    batch_rows, length_tok, width_ff = activations.shape
    width_model = out_grads.shape[2]
    rank = proj_in.shape[1]
    entries = test_grads.shape[1]
    act_part = jnp.dot(
        activations.reshape(-1, width_ff), proj_in, preferred_element_type=jnp.float32
    ).reshape(batch_rows, length_tok, -1)
    grad_part = jnp.dot(
        out_grads.reshape(-1, width_model), proj_out, preferred_element_type=jnp.float32
    ).reshape(batch_rows, length_tok, -1)
    paired = jnp.concatenate([grad_part, act_part], axis=2)
    summed = lax.psum_scatter(paired, "tensor", scatter_dimension=1, tiled=True)
    products = jnp.einsum(
        "eto,eti->eoi", summed[:, :, :rank], summed[:, :, rank:], precision=HIGH
    )
    partial = products.reshape(batch_rows, entries) / LEN
    pieces = lax.all_gather(partial, ("tensor", "dp"), axis=0, tiled=True)
    gradients = jnp.sum(pieces.reshape(lax.axis_size("tensor"), -1, entries), axis=0)
    rows_here = fisher_prior.shape[0]
    offset = lax.axis_index("tensor") * rows_here
    residual = test_grads
    direction = residual
    solution = jnp.zeros_like(residual)
    norm_now = jnp.sum(residual * residual, axis=1)
    for iteration in range(ITERS):
        image = lax.dot_general(direction, fisher_prior, CONTRACT, precision=HIGH)
        image = lax.all_gather(image, "tensor", axis=1, tiled=True)
        coeffs = lax.dot_general(direction, gradients, CONTRACT, precision=HIGH)
        low = jnp.dot(coeffs, gradients, precision=HIGH)
        applied = image + low + DAMPING * direction
        step_size = norm_now / jnp.sum(direction * applied, axis=1)
        solution = solution + step_size[:, None] * direction
        if iteration + 1 < ITERS:
            residual = residual - step_size[:, None] * applied
            norm_next = jnp.sum(residual * residual, axis=1)
            direction = residual + (norm_next / norm_now)[:, None] * direction
            norm_now = norm_next
    own = lax.dynamic_slice_in_dim(solution, offset, rows_here, 1)
    scores = lax.dot_general(solution, gradients, CONTRACT, precision=HIGH)
    full = lax.all_gather(own, "dp", axis=0, tiled=True)
    table = lax.all_gather(scores, "dp", axis=0, tiled=True)
    start = lax.axis_index("dp") * batch_rows
    return (lax.dynamic_slice_in_dim(table, start, batch_rows, 1).T, full)


def solution(mesh):
    return jax.shard_map(
        shards,
        mesh=mesh,
        in_specs=(
            P(("parts", "dp"), None, "tensor"),
            P(("parts", "dp"), None, "tensor"),
            P("tensor", None),
            P("tensor", None),
            P("tensor", None),
            P(("parts", "dp"), None),
        ),
        out_specs=(P(("parts", "dp"), None), P("parts", "tensor")),
        check_vma=False,
    )
```

```python
import functools

import jax
import jax.numpy as jnp
from jax import lax
from jax.experimental import pallas as pl
from jax.experimental.pallas import tpu as pltpu
from jax.sharding import PartitionSpec as P

LEN = 512
ITERS = 4
DAMPING = 0.1
CONTRACT = (((1,), (1,)), ((), ()))
HIGH = lax.Precision.HIGH

LANES = 128
STAGE = 128
SLOTS = 4
CHUNK = 256


def split(values):
    high = values.astype(jnp.bfloat16)
    return high, (values - high.astype(jnp.float32)).astype(jnp.bfloat16)


def dot3(left, right, dims):
    a_high, a_low = split(left)
    b_high, b_low = split(right)
    dot = functools.partial(
        lax.dot_general, dimension_numbers=dims, preferred_element_type=jnp.float32
    )
    return dot(a_high, b_high) + (dot(a_low, b_high) + dot(a_high, b_low))


def solve_kernel(
    groups, examples, prior, grads_in, tests_in, full_out, table_out,
    high, low, stage, partner_grads, all_grads, grads, tests, residual, direction,
    solved, images, full, table,
    stage_sem, pair_send, pair_recv, test_send, test_recv, cast_send, cast_recv,
    image_send, image_recv, full_send, full_recv, pass_send, pass_recv,
    table_send, table_recv,
):
    x = lax.axis_index("tensor")
    k = lax.axis_index("dp")
    z, c = k // 2, lax.rem(k, 2)
    chips = groups // 2
    rows, entries = tests_in.shape
    wide = 2 * rows
    quarter = high.shape[0]
    half = 2 * quarter
    block = grads_in.shape[0]
    across, sibling = lax.rem(x + 1, 2), z * 2 + lax.rem(c + 1, 2)

    def push(source, target, send, recv, tensor, dp):
        return pltpu.make_async_remote_copy(
            src_ref=source, dst_ref=target, send_sem=send, recv_sem=recv,
            device_id={"tensor": tensor, "dp": dp},
            device_id_type=pl.DeviceIdType.MESH,
        )

    quad = [(across, k), (x, sibling), (across, sibling)]
    far = [(lax.rem(z + step, chips)) for step in range(1, chips)]
    back = [(lax.rem(z + chips - step, chips)) for step in range(1, chips)]

    def load(index):
        slot = lax.rem(index, SLOTS)
        start = pl.multiple_of(c * quarter + index * STAGE, STAGE)
        return pltpu.make_async_copy(
            prior.at[pl.ds(start, STAGE), :], stage.at[slot], stage_sem.at[slot]
        )

    count = quarter // STAGE
    for index in range(min(SLOTS - 1, count)):
        load(index).start()

    barrier = pltpu.get_barrier_semaphore()
    peers = quad + [(x, chip * 2 + core) for chip in far for core in range(2)]
    for tensor, dp in peers:
        pl.semaphore_signal(
            barrier, inc=1, device_id={"tensor": tensor, "dp": dp},
            device_id_type=pl.DeviceIdType.MESH,
        )
    pl.semaphore_wait(barrier, len(peers))

    to_pair = push(grads_in, partner_grads, pair_send, pair_recv, across, k)
    to_pair.start()
    mine = tests.at[pl.ds(pl.multiple_of(c * rows, rows), rows), :]
    other = tests.at[pl.ds(pl.multiple_of((1 - c) * rows, rows), rows), :]
    to_sibling = push(tests_in, mine, test_send, test_recv, x, sibling)
    to_sibling.start()
    mine[...] = tests_in[...]

    own = pl.ds(pl.multiple_of(k * block, 8), block)
    to_pair.wait()
    all_grads[own, :] = grads_in[...] + partner_grads[...]
    casts = []
    for step in range(1, groups):
        cast = push(
            all_grads.at[own, :], all_grads.at[own, :], cast_send.at[step - 1],
            cast_recv.at[step - 1], x, lax.rem(k + step, groups),
        )
        cast.start()
        casts.append(cast)

    def take(index, carry):
        @pl.when(index + SLOTS - 1 < count)
        def _():
            load(index + SLOTS - 1).start()

        load(index).wait()
        rows_here = pl.ds(pl.multiple_of(index * STAGE, STAGE), STAGE)
        part_high, part_low = split(stage[lax.rem(index, SLOTS)])
        high[rows_here, :] = part_high
        low[rows_here, :] = part_low
        return carry

    lax.fori_loop(0, count, take, 0)

    to_sibling.wait_send()
    push(tests_in, other, test_send, test_recv, x, sibling).wait_recv()
    start = tests[...]
    residual[...] = start
    direction[...] = start
    solved[...] = jnp.zeros_like(start)
    norm = jnp.sum(start * start, axis=1, keepdims=True)

    chunks = quarter // CHUNK

    def column(tensor, core, chunk):
        first = tensor * half + core * quarter + chunk * CHUNK
        return pl.ds(pl.multiple_of(first, CHUNK), CHUNK)

    def sends(iteration, chunk, send_only=False):
        area = images.at[iteration, :, column(x, c, chunk)]
        return [
            push(area, area, image_send.at[peer, chunk],
                 image_recv.at[iteration, peer, chunk], *quad[peer])
            for peer in range(3)
        ]

    def multiply(iteration):
        d_high, d_low = split(direction[...])
        both = jnp.concatenate([d_high, d_low], axis=0)

        def body(chunk, carry):
            here = pl.ds(pl.multiple_of(chunk * CHUNK, CHUNK), CHUNK)
            first = lax.dot_general(
                both, high[here, :], CONTRACT, preferred_element_type=jnp.float32
            )
            second = lax.dot_general(
                d_high, low[here, :], CONTRACT, preferred_element_type=jnp.float32
            )
            images[iteration, :, column(x, c, chunk)] = first[:wide] + (
                first[wide:] + second
            )
            for copy in sends(iteration, chunk):
                copy.start()
            return carry

        lax.fori_loop(0, chunks, body, 0)

    def finish(iteration):
        cores = [(across, c), (x, 1 - c), (across, 1 - c)]

        def body(chunk, carry):
            for peer in range(3):
                area = images.at[iteration, :, column(*cores[peer], chunk)]
                push(area, area, image_send.at[peer, chunk],
                     image_recv.at[iteration, peer, chunk], *quad[peer]).wait_recv()
            for copy in sends(iteration, chunk):
                copy.wait_send()
            return carry

        lax.fori_loop(0, chunks, body, 0)

    def update(iteration, norm):
        toward = direction[...]
        coeffs = dot3(toward, grads[...], CONTRACT)
        shift = dot3(coeffs, grads[...], (((1,), (0,)), ((), ())))
        finish(iteration)
        applied = images[iteration] + shift + DAMPING * toward
        step = norm / jnp.sum(toward * applied, axis=1, keepdims=True)
        solved[...] = solved[...] + step * toward
        left = residual[...] - step * applied
        residual[...] = left
        fresh = jnp.sum(left * left, axis=1, keepdims=True)
        direction[...] = left + (fresh / norm) * toward
        return fresh

    multiply(0)
    for step in range(1, groups):
        casts[step - 1].wait_send()
        source = lax.rem(k + groups - step, groups)
        area = all_grads.at[pl.ds(pl.multiple_of(source * block, 8), block), :]
        push(area, area, cast_send.at[step - 1], cast_recv.at[step - 1],
             x, source).wait_recv()
    lines = entries // LANES
    grads[...] = jnp.zeros_like(grads)
    for line in range(lines):
        grads[0:examples, line * LANES:(line + 1) * LANES] = all_grads[
            pl.ds(line, examples, stride=lines), :
        ]
    norm = update(0, norm)

    def iterate(iteration, norm):
        multiply(iteration)
        return update(iteration, norm)

    lax.fori_loop(1, ITERS, iterate, norm)

    columns = pl.ds(pl.multiple_of(x * half, half), half)
    ours = solved.at[pl.ds(pl.multiple_of(c * rows, rows), rows), columns]
    place = lambda group: full.at[pl.ds(pl.multiple_of(group * rows, rows), rows), :]
    outgoing = []
    for step in range(chips - 1):
        copy = push(ours, place(k), full_send.at[step], full_recv.at[step],
                    x, far[step] * 2 + c)
        copy.start()
        outgoing.append(copy)
    scores = dot3(grads[...], solved[...], CONTRACT)
    table[z] = jnp.concatenate(
        [scores, jnp.zeros((scores.shape[0], LANES - wide), jnp.float32)], axis=1
    )
    for step in range(chips - 1):
        copy = push(table.at[z], table.at[z], table_send.at[step],
                    table_recv.at[step], x, far[step] * 2 + c)
        copy.start()
        outgoing.append(copy)
    full[pl.ds(pl.multiple_of(z * wide, wide), wide), :] = solved[:, columns]
    for step in range(chips - 1):
        area = place(back[step] * 2 + c)
        push(area, area, full_send.at[step], full_recv.at[step],
             x, back[step] * 2 + c).wait_recv()
        copy = push(area, area, pass_send.at[step], pass_recv.at[step], x, sibling)
        copy.start()
        outgoing.append(copy)
    for step in range(chips - 1):
        area = place(back[step] * 2 + (1 - c))
        push(area, area, pass_send.at[step], pass_recv.at[step],
             x, sibling).wait_recv()
        area = table.at[back[step]]
        push(area, area, table_send.at[step], table_recv.at[step],
             x, back[step] * 2 + c).wait_recv()
    for copy in outgoing:
        copy.wait_send()
    full_out[...] = full[...]
    table_out[...] = table[...]


def solve(prior, partial, test_grads):
    groups = lax.axis_size("dp")
    chips = groups // 2
    rows, entries = test_grads.shape
    half = prior.shape[0]
    quarter = half // 2
    batch_rows = partial.shape[0] * LANES // entries
    block = partial.shape[0]
    examples = groups * batch_rows
    padded = -(-examples // 16) * 16
    f32 = jnp.float32
    vmem = pl.BlockSpec(memory_space=pltpu.VMEM)
    dma = pltpu.SemaphoreType.DMA
    chunks = quarter // CHUNK
    wide = 2 * rows
    work = pltpu.VMEM((wide, entries), f32)
    return pl.pallas_call(
        functools.partial(solve_kernel, groups, examples),
        out_shape=(
            jax.ShapeDtypeStruct((groups * rows, half), f32),
            jax.ShapeDtypeStruct((chips, padded, LANES), f32),
        ),
        in_specs=[pl.BlockSpec(memory_space=pl.ANY), vmem, vmem],
        out_specs=(vmem, vmem),
        scratch_shapes=[
            pltpu.VMEM((quarter, entries), jnp.bfloat16),
            pltpu.VMEM((quarter, entries), jnp.bfloat16),
            pltpu.VMEM((SLOTS, STAGE, entries), f32),
            pltpu.VMEM((block, LANES), f32),
            pltpu.VMEM((groups * block, LANES), f32),
            pltpu.VMEM((padded, entries), f32),
            work, work, work, work,
            pltpu.VMEM((ITERS, wide, entries), f32),
            pltpu.VMEM((groups * rows, half), f32),
            pltpu.VMEM((chips, padded, LANES), f32),
            dma((SLOTS,)), dma, dma, dma, dma,
            dma((groups - 1,)), dma((groups - 1,)),
            dma((3, chunks)), dma((ITERS, 3, chunks)),
            dma((chips - 1,)), dma((chips - 1,)),
            dma((chips - 1,)), dma((chips - 1,)),
            dma((chips - 1,)), dma((chips - 1,)),
        ],
        compiler_params=pltpu.CompilerParams(
            collective_id=0, has_side_effects=True, vmem_limit_bytes=56 * 1024 * 1024
        ),
    )(prior, partial, test_grads)


def shards(activations, out_grads, proj_in, proj_out, fisher_prior, test_grads):
    batch_rows, length_tok, width_ff = activations.shape
    width_model = out_grads.shape[2]
    rank = proj_in.shape[1]
    entries = test_grads.shape[1]
    act_part = jnp.dot(
        activations.reshape(-1, width_ff), proj_in, preferred_element_type=jnp.float32
    ).reshape(batch_rows, length_tok, -1)
    grad_part = jnp.dot(
        out_grads.reshape(-1, width_model), proj_out, preferred_element_type=jnp.float32
    ).reshape(batch_rows, length_tok, -1)
    paired = jnp.concatenate([grad_part, act_part], axis=2)
    summed = lax.psum_scatter(paired, "tensor", scatter_dimension=1, tiled=True)
    products = jnp.einsum(
        "eto,eti->eoi", summed[:, :, :rank], summed[:, :, rank:], precision=HIGH
    )
    partial = products.reshape(batch_rows, entries) / LEN
    if lax.axis_size("tensor") == 2:
        full, table = solve(fisher_prior, partial.reshape(-1, LANES), test_grads)
        start = lax.axis_index("dp") * batch_rows
        mine = lax.dynamic_slice_in_dim(table, start, batch_rows, 1)
        mine = mine[:, :, : 2 * test_grads.shape[0]]
        return (mine.transpose(1, 0, 2).reshape(batch_rows, -1), full)
    pieces = lax.all_gather(partial, ("tensor", "dp"), axis=0, tiled=True)
    gradients = jnp.sum(pieces.reshape(lax.axis_size("tensor"), -1, entries), axis=0)
    rows_here = fisher_prior.shape[0]
    offset = lax.axis_index("tensor") * rows_here
    residual = test_grads
    direction = residual
    solution = jnp.zeros_like(residual)
    norm_now = jnp.sum(residual * residual, axis=1)
    for iteration in range(ITERS):
        image = lax.dot_general(direction, fisher_prior, CONTRACT, precision=HIGH)
        image = lax.all_gather(image, "tensor", axis=1, tiled=True)
        coeffs = lax.dot_general(direction, gradients, CONTRACT, precision=HIGH)
        low = jnp.dot(coeffs, gradients, precision=HIGH)
        applied = image + low + DAMPING * direction
        step_size = norm_now / jnp.sum(direction * applied, axis=1)
        solution = solution + step_size[:, None] * direction
        if iteration + 1 < ITERS:
            residual = residual - step_size[:, None] * applied
            norm_next = jnp.sum(residual * residual, axis=1)
            direction = residual + (norm_next / norm_now)[:, None] * direction
            norm_now = norm_next
    own = lax.dynamic_slice_in_dim(solution, offset, rows_here, 1)
    scores = lax.dot_general(solution, gradients, CONTRACT, precision=HIGH)
    full = lax.all_gather(own, "dp", axis=0, tiled=True)
    table = lax.all_gather(scores, "dp", axis=0, tiled=True)
    start = lax.axis_index("dp") * batch_rows
    return (lax.dynamic_slice_in_dim(table, start, batch_rows, 1).T, full)


def solution(mesh):
    return jax.shard_map(
        shards,
        mesh=mesh,
        in_specs=(
            P(("parts", "dp"), None, "tensor"),
            P(("parts", "dp"), None, "tensor"),
            P("tensor", None),
            P("tensor", None),
            P("tensor", None),
            P(("parts", "dp"), None),
        ),
        out_specs=(P(("parts", "dp"), None), P("parts", "tensor")),
        check_vma=False,
    )
```

```python
import functools

import jax
import jax.numpy as jnp
from jax import lax
from jax.experimental import pallas as pl
from jax.experimental.pallas import tpu as pltpu
from jax.sharding import PartitionSpec as P

LEN = 512
ITERS = 4
DAMPING = 0.1
CONTRACT = (((1,), (1,)), ((), ()))
HIGH = lax.Precision.HIGH

LANES = 128
STAGE = 64
SLOTS = 4
TOKEN_SLOTS = 3
CHUNK = 256


def split(values):
    high = values.astype(jnp.bfloat16)
    return high, (values - high.astype(jnp.float32)).astype(jnp.bfloat16)


def dot3(left, right, dims):
    a_high, a_low = split(left)
    b_high, b_low = split(right)
    dot = functools.partial(
        lax.dot_general, dimension_numbers=dims, preferred_element_type=jnp.float32
    )
    return dot(a_high, b_high) + (dot(a_low, b_high) + dot(a_high, b_low))


def solve_kernel(
    groups, examples, length, hidden_in, model_in, prior, basis_in, basis_out, tests_in,
    full_out, table_out,
    hidden, model, parts, incoming, mixed, grads_in,
    high, low, stage, partner_grads, all_grads, grads, tests, residual, direction,
    solved, images, full, table,
    token_sem, part_send, part_recv, stage_sem, pair_send, pair_recv, test_send, test_recv, cast_send, cast_recv,
    image_send, image_recv, full_send, full_recv, pass_send, pass_recv,
    table_send, table_recv,
):
    x = lax.axis_index("tensor")
    k = lax.axis_index("dp")
    z, c = k // 2, lax.rem(k, 2)
    chips = groups // 2
    rows, entries = tests_in.shape
    wide = 2 * rows
    quarter = high.shape[0]
    half = 2 * quarter
    block = grads_in.shape[0]
    across, sibling = lax.rem(x + 1, 2), z * 2 + lax.rem(c + 1, 2)

    def push(source, target, send, recv, tensor, dp):
        return pltpu.make_async_remote_copy(
            src_ref=source, dst_ref=target, send_sem=send, recv_sem=recv,
            device_id={"tensor": tensor, "dp": dp},
            device_id_type=pl.DeviceIdType.MESH,
        )

    quad = [(across, k), (x, sibling), (across, sibling)]
    far = [(lax.rem(z + step, chips)) for step in range(1, chips)]
    back = [(lax.rem(z + chips - step, chips)) for step in range(1, chips)]

    def load(index):
        slot = lax.rem(index, SLOTS)
        start = pl.multiple_of(c * quarter + index * STAGE, STAGE)
        return pltpu.make_async_copy(
            prior.at[pl.ds(start, STAGE), :], stage.at[slot], stage_sem.at[slot]
        )

    count = quarter // STAGE
    for index in range(min(SLOTS - 1, count)):
        load(index).start()

    barrier = pltpu.get_barrier_semaphore()
    peers = quad + [(x, chip * 2 + core) for chip in far for core in range(2)]
    for tensor, dp in peers:
        pl.semaphore_signal(
            barrier, inc=1, device_id={"tensor": tensor, "dp": dp},
            device_id_type=pl.DeviceIdType.MESH,
        )
    pl.semaphore_wait(barrier, len(peers))

    mine = tests.at[pl.ds(pl.multiple_of(c * rows, rows), rows), :]
    other = tests.at[pl.ds(pl.multiple_of((1 - c) * rows, rows), rows), :]
    to_sibling = push(tests_in, mine, test_send, test_recv, x, sibling)
    to_sibling.start()
    mine[...] = tests_in[...]

    batch = parts.shape[0] // 2
    rank = basis_in.shape[0]
    span = length // 2
    steps = 2 * batch

    def fetch(index):
        turn = index // batch
        first = (index - turn * batch) * length + lax.rem(across + turn, 2) * span
        tokens = pl.ds(pl.multiple_of(first, span), span)
        slot = lax.rem(index, TOKEN_SLOTS)
        return [
            pltpu.make_async_copy(
                hidden_in.at[tokens, :], hidden.at[slot], token_sem.at[0, slot]
            ),
            pltpu.make_async_copy(
                model_in.at[tokens, :], model.at[slot], token_sem.at[1, slot]
            ),
        ]

    def pair_part(example):
        return push(
            parts.at[example], incoming.at[example], part_send.at[example],
            part_recv.at[example], across, k,
        )

    for index in range(min(TOKEN_SLOTS - 1, steps)):
        for copy in fetch(index):
            copy.start()

    def project(index, carry):
        @pl.when(index + TOKEN_SLOTS - 1 < steps)
        def _():
            for copy in fetch(index + TOKEN_SLOTS - 1):
                copy.start()

        for copy in fetch(index):
            copy.wait()
        slot = lax.rem(index, TOKEN_SLOTS)
        parts[index, 0:rank, :] = lax.dot_general(
            basis_out[...], model[slot], CONTRACT, preferred_element_type=jnp.float32
        )
        parts[index, rank:, :] = lax.dot_general(
            basis_in[...], hidden[slot], CONTRACT, preferred_element_type=jnp.float32
        )

        @pl.when(index < batch)
        def _():
            pair_part(index).start()

        @pl.when(index >= batch)
        def _():
            example = index - batch
            pair_part(example).wait()
            both = parts[index] + incoming[example]
            right = both[rank:]
            mixed[...] = dot3(
                both[:rank], jnp.concatenate([right, right], axis=0), CONTRACT
            )
            pairs = rank // 2
            even = mixed[pl.ds(0, pairs, stride=2), :]
            odd = mixed[pl.ds(1, pairs, stride=2), :]
            lane = lax.broadcasted_iota(jnp.int32, even.shape, 1)
            grads_in[pl.ds(pl.multiple_of(example * pairs, 8), pairs), :] = (
                jnp.where(lane < rank, even, odd) / LEN
            )

        return carry

    lax.fori_loop(0, steps, project, 0)
    to_pair = push(grads_in, partner_grads, pair_send, pair_recv, across, k)
    to_pair.start()
    own = pl.ds(pl.multiple_of(k * block, 8), block)
    to_pair.wait()
    all_grads[own, :] = grads_in[...] + partner_grads[...]
    casts = []
    for step in range(1, groups):
        cast = push(
            all_grads.at[own, :], all_grads.at[own, :], cast_send.at[step - 1],
            cast_recv.at[step - 1], x, lax.rem(k + step, groups),
        )
        cast.start()
        casts.append(cast)

    def take(index, carry):
        @pl.when(index + SLOTS - 1 < count)
        def _():
            load(index + SLOTS - 1).start()

        load(index).wait()
        rows_here = pl.ds(pl.multiple_of(index * STAGE, STAGE), STAGE)
        part_high, part_low = split(stage[lax.rem(index, SLOTS)])
        high[rows_here, :] = part_high
        low[rows_here, :] = part_low
        return carry

    lax.fori_loop(0, count, take, 0)

    to_sibling.wait_send()
    push(tests_in, other, test_send, test_recv, x, sibling).wait_recv()
    start = tests[...]
    residual[...] = start
    direction[...] = start
    solved[...] = jnp.zeros_like(start)
    norm = jnp.sum(start * start, axis=1, keepdims=True)

    chunks = quarter // CHUNK

    def column(tensor, core, chunk):
        first = tensor * half + core * quarter + chunk * CHUNK
        return pl.ds(pl.multiple_of(first, CHUNK), CHUNK)

    def sends(iteration, chunk, send_only=False):
        area = images.at[iteration, :, column(x, c, chunk)]
        return [
            push(area, area, image_send.at[peer, chunk],
                 image_recv.at[iteration, peer, chunk], *quad[peer])
            for peer in range(3)
        ]

    def multiply(iteration):
        d_high, d_low = split(direction[...])
        both = jnp.concatenate([d_high, d_low], axis=0)

        def body(chunk, carry):
            here = pl.ds(pl.multiple_of(chunk * CHUNK, CHUNK), CHUNK)
            first = lax.dot_general(
                both, high[here, :], CONTRACT, preferred_element_type=jnp.float32
            )
            second = lax.dot_general(
                d_high, low[here, :], CONTRACT, preferred_element_type=jnp.float32
            )
            images[iteration, :, column(x, c, chunk)] = first[:wide] + (
                first[wide:] + second
            )
            for copy in sends(iteration, chunk):
                copy.start()
            return carry

        lax.fori_loop(0, chunks, body, 0)

    def finish(iteration):
        cores = [(across, c), (x, 1 - c), (across, 1 - c)]

        def body(chunk, carry):
            for peer in range(3):
                area = images.at[iteration, :, column(*cores[peer], chunk)]
                push(area, area, image_send.at[peer, chunk],
                     image_recv.at[iteration, peer, chunk], *quad[peer]).wait_recv()
            for copy in sends(iteration, chunk):
                copy.wait_send()
            return carry

        lax.fori_loop(0, chunks, body, 0)

    def update(iteration, norm):
        toward = direction[...]
        coeffs = dot3(toward, grads[...], CONTRACT)
        shift = dot3(coeffs, grads[...], (((1,), (0,)), ((), ())))
        finish(iteration)
        applied = images[iteration] + shift + DAMPING * toward
        step = norm / jnp.sum(toward * applied, axis=1, keepdims=True)
        solved[...] = solved[...] + step * toward
        left = residual[...] - step * applied
        residual[...] = left
        fresh = jnp.sum(left * left, axis=1, keepdims=True)
        direction[...] = left + (fresh / norm) * toward
        return fresh

    multiply(0)
    for step in range(1, groups):
        casts[step - 1].wait_send()
        source = lax.rem(k + groups - step, groups)
        area = all_grads.at[pl.ds(pl.multiple_of(source * block, 8), block), :]
        push(area, area, cast_send.at[step - 1], cast_recv.at[step - 1],
             x, source).wait_recv()
    lines = entries // LANES
    grads[...] = jnp.zeros_like(grads)
    for line in range(lines):
        grads[0:examples, line * LANES:(line + 1) * LANES] = all_grads[
            pl.ds(line, examples, stride=lines), :
        ]
    norm = update(0, norm)

    def iterate(iteration, norm):
        multiply(iteration)
        return update(iteration, norm)

    lax.fori_loop(1, ITERS, iterate, norm)

    columns = pl.ds(pl.multiple_of(x * half, half), half)
    ours = solved.at[pl.ds(pl.multiple_of(c * rows, rows), rows), columns]
    place = lambda group: full.at[pl.ds(pl.multiple_of(group * rows, rows), rows), :]
    outgoing = []
    for step in range(chips - 1):
        copy = push(ours, place(k), full_send.at[step], full_recv.at[step],
                    x, far[step] * 2 + c)
        copy.start()
        outgoing.append(copy)
    scores = dot3(grads[...], solved[...], CONTRACT)
    table[z] = jnp.concatenate(
        [scores, jnp.zeros((scores.shape[0], LANES - wide), jnp.float32)], axis=1
    )
    for step in range(chips - 1):
        copy = push(table.at[z], table.at[z], table_send.at[step],
                    table_recv.at[step], x, far[step] * 2 + c)
        copy.start()
        outgoing.append(copy)
    full[pl.ds(pl.multiple_of(z * wide, wide), wide), :] = solved[:, columns]
    for step in range(chips - 1):
        area = place(back[step] * 2 + c)
        push(area, area, full_send.at[step], full_recv.at[step],
             x, back[step] * 2 + c).wait_recv()
        copy = push(area, area, pass_send.at[step], pass_recv.at[step], x, sibling)
        copy.start()
        outgoing.append(copy)
    for step in range(chips - 1):
        area = place(back[step] * 2 + (1 - c))
        push(area, area, pass_send.at[step], pass_recv.at[step],
             x, sibling).wait_recv()
        area = table.at[back[step]]
        push(area, area, table_send.at[step], table_recv.at[step],
             x, back[step] * 2 + c).wait_recv()
    for copy in outgoing:
        copy.wait_send()
    full_out[...] = full[...]
    table_out[...] = table[...]


def solve(activations, out_grads, proj_in, proj_out, prior, test_grads):
    groups = lax.axis_size("dp")
    chips = groups // 2
    rows, entries = test_grads.shape
    half = prior.shape[0]
    quarter = half // 2
    batch_rows, length, width_ff = activations.shape
    width_model = out_grads.shape[2]
    rank = proj_in.shape[1]
    block = batch_rows * entries // LANES
    span = length // 2
    examples = groups * batch_rows
    padded = -(-examples // 16) * 16
    f32 = jnp.float32
    vmem = pl.BlockSpec(memory_space=pltpu.VMEM)
    dma = pltpu.SemaphoreType.DMA
    chunks = quarter // CHUNK
    wide = 2 * rows
    work = pltpu.VMEM((wide, entries), f32)
    return pl.pallas_call(
        functools.partial(solve_kernel, groups, examples, length),
        out_shape=(
            jax.ShapeDtypeStruct((groups * rows, half), f32),
            jax.ShapeDtypeStruct((chips, padded, LANES), f32),
        ),
        in_specs=[pl.BlockSpec(memory_space=pl.ANY)] * 3 + [vmem] * 3,
        out_specs=(vmem, vmem),
        scratch_shapes=[
            pltpu.VMEM((TOKEN_SLOTS, span, width_ff), jnp.bfloat16),
            pltpu.VMEM((TOKEN_SLOTS, span, width_model), jnp.bfloat16),
            pltpu.VMEM((2 * batch_rows, 2 * rank, span), f32),
            pltpu.VMEM((batch_rows, 2 * rank, span), f32),
            pltpu.VMEM((rank, LANES), f32),
            pltpu.VMEM((block, LANES), f32),
            pltpu.VMEM((quarter, entries), jnp.bfloat16),
            pltpu.VMEM((quarter, entries), jnp.bfloat16),
            pltpu.VMEM((SLOTS, STAGE, entries), f32),
            pltpu.VMEM((block, LANES), f32),
            pltpu.VMEM((groups * block, LANES), f32),
            pltpu.VMEM((padded, entries), f32),
            work, work, work, work,
            pltpu.VMEM((ITERS, wide, entries), f32),
            pltpu.VMEM((groups * rows, half), f32),
            pltpu.VMEM((chips, padded, LANES), f32),
            dma((2, TOKEN_SLOTS)), dma((batch_rows,)), dma((batch_rows,)),
            dma((SLOTS,)), dma, dma, dma, dma,
            dma((groups - 1,)), dma((groups - 1,)),
            dma((3, chunks)), dma((ITERS, 3, chunks)),
            dma((chips - 1,)), dma((chips - 1,)),
            dma((chips - 1,)), dma((chips - 1,)),
            dma((chips - 1,)), dma((chips - 1,)),
        ],
        compiler_params=pltpu.CompilerParams(
            collective_id=0, has_side_effects=True, vmem_limit_bytes=62 * 1024 * 1024
        ),
    )(
        activations.reshape(-1, width_ff), out_grads.reshape(-1, width_model), prior,
        proj_in.T, proj_out.T, test_grads,
    )


def shards(activations, out_grads, proj_in, proj_out, fisher_prior, test_grads):
    batch_rows, length_tok, width_ff = activations.shape
    width_model = out_grads.shape[2]
    rank = proj_in.shape[1]
    entries = test_grads.shape[1]
    if lax.axis_size("tensor") == 2 and 2 * rank == LANES:
        full, table = solve(
            activations, out_grads, proj_in, proj_out, fisher_prior, test_grads
        )
        start = lax.axis_index("dp") * batch_rows
        mine = lax.dynamic_slice_in_dim(table, start, batch_rows, 1)
        mine = mine[:, :, : 2 * test_grads.shape[0]]
        return (mine.transpose(1, 0, 2).reshape(batch_rows, -1), full)
    act_part = jnp.dot(
        activations.reshape(-1, width_ff), proj_in, preferred_element_type=jnp.float32
    ).reshape(batch_rows, length_tok, -1)
    grad_part = jnp.dot(
        out_grads.reshape(-1, width_model), proj_out, preferred_element_type=jnp.float32
    ).reshape(batch_rows, length_tok, -1)
    paired = jnp.concatenate([grad_part, act_part], axis=2)
    summed = lax.psum_scatter(paired, "tensor", scatter_dimension=1, tiled=True)
    products = jnp.einsum(
        "eto,eti->eoi", summed[:, :, :rank], summed[:, :, rank:], precision=HIGH
    )
    partial = products.reshape(batch_rows, entries) / LEN
    pieces = lax.all_gather(partial, ("tensor", "dp"), axis=0, tiled=True)
    gradients = jnp.sum(pieces.reshape(lax.axis_size("tensor"), -1, entries), axis=0)
    rows_here = fisher_prior.shape[0]
    offset = lax.axis_index("tensor") * rows_here
    residual = test_grads
    direction = residual
    solution = jnp.zeros_like(residual)
    norm_now = jnp.sum(residual * residual, axis=1)
    for iteration in range(ITERS):
        image = lax.dot_general(direction, fisher_prior, CONTRACT, precision=HIGH)
        image = lax.all_gather(image, "tensor", axis=1, tiled=True)
        coeffs = lax.dot_general(direction, gradients, CONTRACT, precision=HIGH)
        low = jnp.dot(coeffs, gradients, precision=HIGH)
        applied = image + low + DAMPING * direction
        step_size = norm_now / jnp.sum(direction * applied, axis=1)
        solution = solution + step_size[:, None] * direction
        if iteration + 1 < ITERS:
            residual = residual - step_size[:, None] * applied
            norm_next = jnp.sum(residual * residual, axis=1)
            direction = residual + (norm_next / norm_now)[:, None] * direction
            norm_now = norm_next
    own = lax.dynamic_slice_in_dim(solution, offset, rows_here, 1)
    scores = lax.dot_general(solution, gradients, CONTRACT, precision=HIGH)
    full = lax.all_gather(own, "dp", axis=0, tiled=True)
    table = lax.all_gather(scores, "dp", axis=0, tiled=True)
    start = lax.axis_index("dp") * batch_rows
    return (lax.dynamic_slice_in_dim(table, start, batch_rows, 1).T, full)


def solution(mesh):
    return jax.shard_map(
        shards,
        mesh=mesh,
        in_specs=(
            P(("parts", "dp"), None, "tensor"),
            P(("parts", "dp"), None, "tensor"),
            P("tensor", None),
            P("tensor", None),
            P("tensor", None),
            P(("parts", "dp"), None),
        ),
        out_specs=(P(("parts", "dp"), None), P("parts", "tensor")),
        check_vma=False,
    )
```

```python
import functools

import jax
import jax.numpy as jnp
from jax import lax
from jax.experimental import pallas as pl
from jax.experimental.pallas import tpu as pltpu
from jax.sharding import PartitionSpec as P

LEN = 512
ITERS = 4
DAMPING = 0.1
CONTRACT = (((1,), (1,)), ((), ()))
HIGH = lax.Precision.HIGH

LANES = 128
STAGE = 64
SLOTS = 4
TOKEN_SLOTS = 3
CHUNK = 256


def split(values):
    high = values.astype(jnp.bfloat16)
    return high, (values - high.astype(jnp.float32)).astype(jnp.bfloat16)


def dot3(left, right, dims):
    a_high, a_low = split(left)
    b_high, b_low = split(right)
    dot = functools.partial(
        lax.dot_general, dimension_numbers=dims, preferred_element_type=jnp.float32
    )
    return dot(a_high, b_high) + (dot(a_low, b_high) + dot(a_high, b_low))


def solve_kernel(
    groups, examples, length, hidden_in, model_in, prior, basis_in, basis_out, tests_in,
    full_out, table_out,
    hidden, model, parts, incoming, mixed, grads_in,
    high, low, stage, partner_grads, all_grads, grads, tests, residual, direction,
    solved, images, full, table,
    token_sem, part_send, part_recv, stage_sem, pair_send, pair_recv, test_send, test_recv, cast_send, cast_recv,
    image_send, image_recv, full_send, full_recv, pass_send, pass_recv,
    table_send, table_recv,
):
    x = lax.axis_index("tensor")
    k = lax.axis_index("dp")
    z, c = k // 2, lax.rem(k, 2)
    chips = groups // 2
    rows, entries = tests_in.shape
    wide = 2 * rows
    quarter = high.shape[0]
    half = 2 * quarter
    block = grads_in.shape[0]
    across, sibling = lax.rem(x + 1, 2), z * 2 + lax.rem(c + 1, 2)

    def push(source, target, send, recv, tensor, dp):
        return pltpu.make_async_remote_copy(
            src_ref=source, dst_ref=target, send_sem=send, recv_sem=recv,
            device_id={"tensor": tensor, "dp": dp},
            device_id_type=pl.DeviceIdType.MESH,
        )

    quad = [(across, k), (x, sibling), (across, sibling)]
    far = [(lax.rem(z + step, chips)) for step in range(1, chips)]
    back = [(lax.rem(z + chips - step, chips)) for step in range(1, chips)]

    def load(index):
        slot = lax.rem(index, SLOTS)
        start = pl.multiple_of(c * quarter + index * STAGE, STAGE)
        return pltpu.make_async_copy(
            prior.at[pl.ds(start, STAGE), :], stage.at[slot], stage_sem.at[slot]
        )

    count = quarter // STAGE
    for index in range(min(SLOTS - 1, count)):
        load(index).start()

    barrier = pltpu.get_barrier_semaphore()
    peers = quad + [(x, chip * 2 + core) for chip in far for core in range(2)]
    for tensor, dp in peers:
        pl.semaphore_signal(
            barrier, inc=1, device_id={"tensor": tensor, "dp": dp},
            device_id_type=pl.DeviceIdType.MESH,
        )
    pl.semaphore_wait(barrier, len(peers))

    mine = tests.at[pl.ds(pl.multiple_of(c * rows, rows), rows), :]
    other = tests.at[pl.ds(pl.multiple_of((1 - c) * rows, rows), rows), :]
    to_sibling = push(tests_in, mine, test_send, test_recv, x, sibling)
    to_sibling.start()
    mine[...] = tests_in[...]

    batch = parts.shape[0] // 2
    rank = basis_in.shape[0]
    span = length // 2
    steps = 2 * batch

    def fetch(index):
        turn = index // batch
        first = (index - turn * batch) * length + lax.rem(across + turn, 2) * span
        tokens = pl.ds(pl.multiple_of(first, span), span)
        slot = lax.rem(index, TOKEN_SLOTS)
        return [
            pltpu.make_async_copy(
                hidden_in.at[tokens, :], hidden.at[slot], token_sem.at[0, slot]
            ),
            pltpu.make_async_copy(
                model_in.at[tokens, :], model.at[slot], token_sem.at[1, slot]
            ),
        ]

    def pair_part(example):
        return push(
            parts.at[example], incoming.at[example], part_send.at[example],
            part_recv.at[example], across, k,
        )

    for index in range(min(TOKEN_SLOTS - 1, steps)):
        for copy in fetch(index):
            copy.start()

    def project(index, carry):
        @pl.when(index + TOKEN_SLOTS - 1 < steps)
        def _():
            for copy in fetch(index + TOKEN_SLOTS - 1):
                copy.start()

        for copy in fetch(index):
            copy.wait()
        slot = lax.rem(index, TOKEN_SLOTS)
        parts[index, 0:rank, :] = lax.dot_general(
            basis_out[...], model[slot], CONTRACT, preferred_element_type=jnp.float32
        )
        parts[index, rank:, :] = lax.dot_general(
            basis_in[...], hidden[slot], CONTRACT, preferred_element_type=jnp.float32
        )

        @pl.when(index < batch)
        def _():
            pair_part(index).start()

        @pl.when(index >= batch)
        def _():
            example = index - batch
            pair_part(example).wait()
            both = parts[index] + incoming[example]
            right = both[rank:]
            mixed[...] = dot3(
                both[:rank], jnp.concatenate([right, right], axis=0), CONTRACT
            )
            pairs = rank // 2
            even = mixed[pl.ds(0, pairs, stride=2), :]
            odd = mixed[pl.ds(1, pairs, stride=2), :]
            lane = lax.broadcasted_iota(jnp.int32, even.shape, 1)
            grads_in[pl.ds(pl.multiple_of(example * pairs, 8), pairs), :] = (
                jnp.where(lane < rank, even, odd) / LEN
            )

        return carry

    lax.fori_loop(0, steps, project, 0)
    to_pair = push(grads_in, partner_grads, pair_send, pair_recv, across, k)
    to_pair.start()
    def take(index, carry):
        @pl.when(index + SLOTS - 1 < count)
        def _():
            load(index + SLOTS - 1).start()

        load(index).wait()
        rows_here = pl.ds(pl.multiple_of(index * STAGE, STAGE), STAGE)
        part_high, part_low = split(stage[lax.rem(index, SLOTS)])
        high[rows_here, :] = part_high
        low[rows_here, :] = part_low
        return carry

    to_sibling.wait_send()
    push(tests_in, other, test_send, test_recv, x, sibling).wait_recv()
    start = tests[...]
    residual[...] = start
    direction[...] = start
    solved[...] = jnp.zeros_like(start)
    norm = jnp.sum(start * start, axis=1, keepdims=True)

    chunks = quarter // CHUNK

    def column(tensor, core, chunk):
        first = tensor * half + core * quarter + chunk * CHUNK
        return pl.ds(pl.multiple_of(first, CHUNK), CHUNK)

    def sends(iteration, chunk, send_only=False):
        area = images.at[iteration, :, column(x, c, chunk)]
        return [
            push(area, area, image_send.at[peer, chunk],
                 image_recv.at[iteration, peer, chunk], *quad[peer])
            for peer in range(3)
        ]

    def multiply(iteration, first_pass=False):
        d_high, d_low = split(direction[...])
        both = jnp.concatenate([d_high, d_low], axis=0)

        def body(chunk, carry):
            if first_pass:
                lax.fori_loop(chunk * per_chunk, (chunk + 1) * per_chunk, take, 0)
            here = pl.ds(pl.multiple_of(chunk * CHUNK, CHUNK), CHUNK)
            first = lax.dot_general(
                both, high[here, :], CONTRACT, preferred_element_type=jnp.float32
            )
            second = lax.dot_general(
                d_high, low[here, :], CONTRACT, preferred_element_type=jnp.float32
            )
            images[iteration, :, column(x, c, chunk)] = first[:wide] + (
                first[wide:] + second
            )
            for copy in sends(iteration, chunk):
                copy.start()
            return carry

        if first_pass:
            lax.fori_loop(0, 1, body, 0)
            return body
        lax.fori_loop(0, chunks, body, 0)

    def finish(iteration):
        cores = [(across, c), (x, 1 - c), (across, 1 - c)]

        def body(chunk, carry):
            for peer in range(3):
                area = images.at[iteration, :, column(*cores[peer], chunk)]
                push(area, area, image_send.at[peer, chunk],
                     image_recv.at[iteration, peer, chunk], *quad[peer]).wait_recv()
            for copy in sends(iteration, chunk):
                copy.wait_send()
            return carry

        lax.fori_loop(0, chunks, body, 0)

    def update(iteration, norm):
        toward = direction[...]
        coeffs = dot3(toward, grads[...], CONTRACT)
        shift = dot3(coeffs, grads[...], (((1,), (0,)), ((), ())))
        finish(iteration)
        applied = images[iteration] + shift + DAMPING * toward
        step = norm / jnp.sum(toward * applied, axis=1, keepdims=True)
        solved[...] = solved[...] + step * toward
        left = residual[...] - step * applied
        residual[...] = left
        fresh = jnp.sum(left * left, axis=1, keepdims=True)
        direction[...] = left + (fresh / norm) * toward
        return fresh

    per_chunk = CHUNK // STAGE
    remaining = multiply(0, first_pass=True)
    own = pl.ds(pl.multiple_of(k * block, 8), block)
    to_pair.wait()
    all_grads[own, :] = grads_in[...] + partner_grads[...]
    casts = []
    for step in range(1, groups):
        cast = push(
            all_grads.at[own, :], all_grads.at[own, :], cast_send.at[step - 1],
            cast_recv.at[step - 1], x, lax.rem(k + step, groups),
        )
        cast.start()
        casts.append(cast)

    lax.fori_loop(1, chunks, remaining, 0)
    for step in range(1, groups):
        casts[step - 1].wait_send()
        source = lax.rem(k + groups - step, groups)
        area = all_grads.at[pl.ds(pl.multiple_of(source * block, 8), block), :]
        push(area, area, cast_send.at[step - 1], cast_recv.at[step - 1],
             x, source).wait_recv()
    lines = entries // LANES
    grads[...] = jnp.zeros_like(grads)
    for line in range(lines):
        grads[0:examples, line * LANES:(line + 1) * LANES] = all_grads[
            pl.ds(line, examples, stride=lines), :
        ]
    norm = update(0, norm)

    def iterate(iteration, norm):
        multiply(iteration)
        return update(iteration, norm)

    lax.fori_loop(1, ITERS, iterate, norm)

    columns = pl.ds(pl.multiple_of(x * half, half), half)
    ours = solved.at[pl.ds(pl.multiple_of(c * rows, rows), rows), columns]
    place = lambda group: full.at[pl.ds(pl.multiple_of(group * rows, rows), rows), :]
    outgoing = []
    for step in range(chips - 1):
        copy = push(ours, place(k), full_send.at[step], full_recv.at[step],
                    x, far[step] * 2 + c)
        copy.start()
        outgoing.append(copy)
    scores = dot3(grads[...], solved[...], CONTRACT)
    table[z] = jnp.concatenate(
        [scores, jnp.zeros((scores.shape[0], LANES - wide), jnp.float32)], axis=1
    )
    for step in range(chips - 1):
        copy = push(table.at[z], table.at[z], table_send.at[step],
                    table_recv.at[step], x, far[step] * 2 + c)
        copy.start()
        outgoing.append(copy)
    full[pl.ds(pl.multiple_of(z * wide, wide), wide), :] = solved[:, columns]
    for step in range(chips - 1):
        area = place(back[step] * 2 + c)
        push(area, area, full_send.at[step], full_recv.at[step],
             x, back[step] * 2 + c).wait_recv()
        copy = push(area, area, pass_send.at[step], pass_recv.at[step], x, sibling)
        copy.start()
        outgoing.append(copy)
    for step in range(chips - 1):
        area = place(back[step] * 2 + (1 - c))
        push(area, area, pass_send.at[step], pass_recv.at[step],
             x, sibling).wait_recv()
        area = table.at[back[step]]
        push(area, area, table_send.at[step], table_recv.at[step],
             x, back[step] * 2 + c).wait_recv()
    for copy in outgoing:
        copy.wait_send()
    full_out[...] = full[...]
    table_out[...] = table[...]


def solve(activations, out_grads, proj_in, proj_out, prior, test_grads):
    groups = lax.axis_size("dp")
    chips = groups // 2
    rows, entries = test_grads.shape
    half = prior.shape[0]
    quarter = half // 2
    batch_rows, length, width_ff = activations.shape
    width_model = out_grads.shape[2]
    rank = proj_in.shape[1]
    block = batch_rows * entries // LANES
    span = length // 2
    examples = groups * batch_rows
    padded = -(-examples // 16) * 16
    f32 = jnp.float32
    vmem = pl.BlockSpec(memory_space=pltpu.VMEM)
    dma = pltpu.SemaphoreType.DMA
    chunks = quarter // CHUNK
    wide = 2 * rows
    work = pltpu.VMEM((wide, entries), f32)
    return pl.pallas_call(
        functools.partial(solve_kernel, groups, examples, length),
        out_shape=(
            jax.ShapeDtypeStruct((groups * rows, half), f32),
            jax.ShapeDtypeStruct((chips, padded, LANES), f32),
        ),
        in_specs=[pl.BlockSpec(memory_space=pl.ANY)] * 3 + [vmem] * 3,
        out_specs=(vmem, vmem),
        scratch_shapes=[
            pltpu.VMEM((TOKEN_SLOTS, span, width_ff), jnp.bfloat16),
            pltpu.VMEM((TOKEN_SLOTS, span, width_model), jnp.bfloat16),
            pltpu.VMEM((2 * batch_rows, 2 * rank, span), f32),
            pltpu.VMEM((batch_rows, 2 * rank, span), f32),
            pltpu.VMEM((rank, LANES), f32),
            pltpu.VMEM((block, LANES), f32),
            pltpu.VMEM((quarter, entries), jnp.bfloat16),
            pltpu.VMEM((quarter, entries), jnp.bfloat16),
            pltpu.VMEM((SLOTS, STAGE, entries), f32),
            pltpu.VMEM((block, LANES), f32),
            pltpu.VMEM((groups * block, LANES), f32),
            pltpu.VMEM((padded, entries), f32),
            work, work, work, work,
            pltpu.VMEM((ITERS, wide, entries), f32),
            pltpu.VMEM((groups * rows, half), f32),
            pltpu.VMEM((chips, padded, LANES), f32),
            dma((2, TOKEN_SLOTS)), dma((batch_rows,)), dma((batch_rows,)),
            dma((SLOTS,)), dma, dma, dma, dma,
            dma((groups - 1,)), dma((groups - 1,)),
            dma((3, chunks)), dma((ITERS, 3, chunks)),
            dma((chips - 1,)), dma((chips - 1,)),
            dma((chips - 1,)), dma((chips - 1,)),
            dma((chips - 1,)), dma((chips - 1,)),
        ],
        compiler_params=pltpu.CompilerParams(
            collective_id=0, has_side_effects=True, vmem_limit_bytes=62 * 1024 * 1024
        ),
    )(
        activations.reshape(-1, width_ff), out_grads.reshape(-1, width_model), prior,
        proj_in.T, proj_out.T, test_grads,
    )


def shards(activations, out_grads, proj_in, proj_out, fisher_prior, test_grads):
    batch_rows, length_tok, width_ff = activations.shape
    width_model = out_grads.shape[2]
    rank = proj_in.shape[1]
    entries = test_grads.shape[1]
    if lax.axis_size("tensor") == 2 and 2 * rank == LANES:
        full, table = solve(
            activations, out_grads, proj_in, proj_out, fisher_prior, test_grads
        )
        start = lax.axis_index("dp") * batch_rows
        mine = lax.dynamic_slice_in_dim(table, start, batch_rows, 1)
        mine = mine[:, :, : 2 * test_grads.shape[0]]
        return (mine.transpose(1, 0, 2).reshape(batch_rows, -1), full)
    act_part = jnp.dot(
        activations.reshape(-1, width_ff), proj_in, preferred_element_type=jnp.float32
    ).reshape(batch_rows, length_tok, -1)
    grad_part = jnp.dot(
        out_grads.reshape(-1, width_model), proj_out, preferred_element_type=jnp.float32
    ).reshape(batch_rows, length_tok, -1)
    paired = jnp.concatenate([grad_part, act_part], axis=2)
    summed = lax.psum_scatter(paired, "tensor", scatter_dimension=1, tiled=True)
    products = jnp.einsum(
        "eto,eti->eoi", summed[:, :, :rank], summed[:, :, rank:], precision=HIGH
    )
    partial = products.reshape(batch_rows, entries) / LEN
    pieces = lax.all_gather(partial, ("tensor", "dp"), axis=0, tiled=True)
    gradients = jnp.sum(pieces.reshape(lax.axis_size("tensor"), -1, entries), axis=0)
    rows_here = fisher_prior.shape[0]
    offset = lax.axis_index("tensor") * rows_here
    residual = test_grads
    direction = residual
    solution = jnp.zeros_like(residual)
    norm_now = jnp.sum(residual * residual, axis=1)
    for iteration in range(ITERS):
        image = lax.dot_general(direction, fisher_prior, CONTRACT, precision=HIGH)
        image = lax.all_gather(image, "tensor", axis=1, tiled=True)
        coeffs = lax.dot_general(direction, gradients, CONTRACT, precision=HIGH)
        low = jnp.dot(coeffs, gradients, precision=HIGH)
        applied = image + low + DAMPING * direction
        step_size = norm_now / jnp.sum(direction * applied, axis=1)
        solution = solution + step_size[:, None] * direction
        if iteration + 1 < ITERS:
            residual = residual - step_size[:, None] * applied
            norm_next = jnp.sum(residual * residual, axis=1)
            direction = residual + (norm_next / norm_now)[:, None] * direction
            norm_now = norm_next
    own = lax.dynamic_slice_in_dim(solution, offset, rows_here, 1)
    scores = lax.dot_general(solution, gradients, CONTRACT, precision=HIGH)
    full = lax.all_gather(own, "dp", axis=0, tiled=True)
    table = lax.all_gather(scores, "dp", axis=0, tiled=True)
    start = lax.axis_index("dp") * batch_rows
    return (lax.dynamic_slice_in_dim(table, start, batch_rows, 1).T, full)


def solution(mesh):
    return jax.shard_map(
        shards,
        mesh=mesh,
        in_specs=(
            P(("parts", "dp"), None, "tensor"),
            P(("parts", "dp"), None, "tensor"),
            P("tensor", None),
            P("tensor", None),
            P("tensor", None),
            P(("parts", "dp"), None),
        ),
        out_specs=(P(("parts", "dp"), None), P("parts", "tensor")),
        check_vma=False,
    )
```
